512 devices in a mesh: section: 8 (over z_hi, core), peer: 64 (over y, z_lo, x).
Axes of the slice: x: 4, y: 4, z: 16 (z_hi: 4, z_lo: 4; z = z_hi * 4 + z_lo), core: 2. Of those that a mesh axis runs over, the one named last changes fastest.
Arguments:
- hidden_in: bfloat16 [8, 8192, 5120], P('section', 'peer'), may hold values from -6 to 6
- out_grad: bfloat16 [8, 8192, 5120], P('section', 'peer'), may hold values from -16 to 16
- gain: float32 [8, 5120], P('section'), may hold values from 0.5 to 1.5
- w_down: bfloat16 [8, 64, 5120], P('section'), may hold values from -0.078125 to 0.078125
- w_up: bfloat16 [8, 64, 5120], P('section'), may hold values from -0.75 to 0.75
- matching: int32 [8, 64], P('section'), may hold values from 0 to 63, each once within a row
Outputs:
- act_out: bfloat16 [8, 8192, 5120], P('section', 'peer')
- grad_down: float32 [8, 64, 5120], P('section', None, 'peer')
- grad_up: float32 [8, 64, 5120], P('section', None, 'peer')
- grad_gain: float32 [8, 5120], P('section', 'peer')
The draws below stay inside these ranges and needn't reach their ends.
Inputs may be any that keep to these rules, and one draw needn't show every extreme that they name: Every row of matching is a permutation of the 64 peers.
All inputs are finite; a program needn't handle non-finite values.
Results may differ from the reference program's by a relative error of at most 0.0053.
Values may be sent and summed in bfloat16 or wider, within the bound.
No kernel may reach another device: no remote copies, remote signals or barrier semaphores. Data moves between devices by JAX's collectives and lax.ppermute only.
A program may use at most 64 MiB of HBM per device.

```python
import jax
import jax.numpy as jnp
from jax import lax

D = 5120
LATENT = 64
ROWS = 8192
N_SECTION = 8
N_PEER = 64


def strengthened(values, key, source, target, parts, factor):
    def block_of(axis_at):
        return (jnp.arange(values.shape[axis_at]) // (values.shape[axis_at] // parts)).reshape((-1,) + (1,) * (values.ndim - 1 - axis_at))

    one_side = jax.random.permutation(key, parts)[block_of(target)]
    other_side = (block_of(target) + parts // 2) % parts
    return jnp.where((block_of(source) == one_side) | (block_of(source) == other_side), factor * values, values)


def block_levels(own_key, dims, cuts, low, largest):
    loudness = 1.0
    for axis_at, parts in cuts:
        heights = jax.random.uniform(jax.random.fold_in(jax.random.fold_in(own_key, 6), axis_at), (parts,), jnp.float32, low / len(cuts), largest / len(cuts))
        loudness = loudness * jnp.repeat(jnp.exp(heights), dims[axis_at] // parts).reshape((-1,) + (1,) * (len(dims) - 1 - axis_at))
    return loudness


def gaussian(stream_key, shape, deviation, bound, shards=(), held_as=jnp.bfloat16):
    loudness = block_levels(stream_key, shape, shards, -0.22, 0.18) if shards else 1.0
    values = jax.random.normal(stream_key, shape, jnp.float32) * deviation * loudness
    return jnp.minimum(jnp.maximum(values, -bound), bound).astype(held_as)


def gaussian_with(stream_key, dims, spread, reach, shards, heavy, kind=jnp.bfloat16):
    drawn = spread * jax.random.normal(stream_key, dims, jnp.float32)
    if shards:
        drawn = drawn * block_levels(stream_key, dims, shards, -0.22, 0.18)
    return jnp.clip(strengthened(drawn, jax.random.fold_in(stream_key, 3), *heavy), -reach, reach).astype(kind)


def setup_inputs(seed: int = 0) -> dict:
    streams_of = jax.random.split(jax.random.key(seed), 7)
    hidden_in = gaussian(streams_of[0], (N_SECTION, ROWS, D), 1.0, 6.0, ((0, 8), (1, 64)))
    out_grad = gaussian_with(streams_of[1], (N_SECTION, ROWS, D), 1.0, 16.0, ((0, 8), (1, 64)), (1, 2, 64, 4.0))
    gain = jnp.clip(1.0 + 0.1 * jax.random.normal(streams_of[2], (N_SECTION, D), jnp.float32), 0.5, 1.5)
    w_down = gaussian(streams_of[3], (N_SECTION, LATENT, D), D ** -0.5, 0.078125, ((0, 8),))
    w_up = gaussian(streams_of[4], (N_SECTION, LATENT, D), LATENT ** -0.5, 0.75, ((0, 8),))
    matching = jax.vmap(lambda own: jax.random.permutation(own, N_PEER))(jax.random.split(streams_of[5], N_SECTION)).reshape((N_SECTION, N_PEER)).astype(jnp.int32)
    return dict(hidden_in=hidden_in, out_grad=out_grad, gain=gain, w_down=w_down, w_up=w_up, matching=matching)


def section_pass(operands):
    tokens, cotangent, gain_row, down_rows, up_rows = operands
    tokens_f = tokens.astype(jnp.float32)
    inv_rms = lax.rsqrt(lax.optimization_barrier(jnp.mean(tokens_f * tokens_f, axis=-1, keepdims=True)) + 1e-05)
    normed = (tokens_f * inv_rms * gain_row).astype(jnp.bfloat16)
    preact = jnp.dot(normed, down_rows.T, preferred_element_type=jnp.float32)
    active = jax.nn.silu(preact).astype(jnp.bfloat16)
    result = (tokens_f + jnp.dot(active, up_rows, preferred_element_type=jnp.float32)).astype(jnp.bfloat16)
    up_grad = jnp.dot(active.T, cotangent, preferred_element_type=jnp.float32)
    act_grad = jnp.dot(cotangent, up_rows.T, preferred_element_type=jnp.float32)
    sigmoid_pre = jax.nn.sigmoid(preact)
    pre_grad = (act_grad * sigmoid_pre * (1.0 + preact * (1.0 - sigmoid_pre))).astype(jnp.bfloat16)
    down_grad = jnp.dot(pre_grad.T, normed, preferred_element_type=jnp.float32)
    normed_grad = jnp.dot(pre_grad, down_rows, preferred_element_type=jnp.float32)
    gain_grad = lax.optimization_barrier(jnp.sum(normed_grad * tokens_f * inv_rms, axis=0))
    return (result, down_grad, up_grad, gain_grad)

def pick_blocks(stacked, picks):
    return stacked[picks]

def reference(hidden_in, out_grad, gain, w_down, w_up, matching):
    section_count, row_count, width = hidden_in.shape
    peer_count = matching.shape[1]
    blocked = out_grad.reshape(section_count, peer_count, row_count // peer_count, width)
    following = jnp.roll(blocked, -1, axis=0)
    cotangent = jax.vmap(pick_blocks)(following, matching).reshape(section_count, row_count, width)
    result, grad_down, grad_up, grad_gain = lax.map(section_pass, (hidden_in, cotangent, gain, w_down, w_up))
    counting = jnp.arange(peer_count, dtype=jnp.int32)
    inverse = jax.vmap(lambda match_row: jnp.zeros_like(match_row).at[match_row].set(counting))(matching)
    routed = jax.vmap(pick_blocks)(result.reshape(section_count, peer_count, row_count // peer_count, width), inverse)
    act_out = jnp.roll(routed, 1, axis=0).reshape(section_count, row_count, width)
    return (act_out, grad_down, grad_up, grad_gain)
```

```python
import jax
import jax.numpy as jnp
from jax import lax
from jax.experimental import pallas as pl
from jax.experimental.pallas import tpu as pltpu
from jax.sharding import PartitionSpec as P

NX, NY, NZ = 4, 4, 4
N_PEER = NX * NY * NZ
N_SECTION = 8
PLANES = [[y * 16 + z * 4 + x for y in range(NY) for x in range(NX)] for z in range(NZ)]
BF16, F32 = jnp.bfloat16, jnp.float32


def along(value, section_steps, z_steps=0):
    pairs = []
    for s in range(N_SECTION):
        for y in range(NY):
            for z in range(NZ):
                for x in range(NX):
                    source = s * N_PEER + y * 16 + z * 4 + x
                    target = ((s + section_steps) % N_SECTION) * N_PEER + y * 16 + ((z + z_steps) % NZ) * 4 + x
                    pairs.append((source, target))
    return lax.ppermute(value, ("section", "peer"), pairs)


def spread_kernel(match_ref, pieces_ref, out_ref):
    def step(p, carry):
        out_ref[match_ref[p]] = pieces_ref[p]
        return carry

    lax.fori_loop(0, N_PEER, step, 0)


def by_target(match_row, pieces):
    return pl.pallas_call(
        spread_kernel,
        out_shape=jax.ShapeDtypeStruct(pieces.shape, pieces.dtype),
        in_specs=[pl.BlockSpec(memory_space=pltpu.SMEM), pl.BlockSpec(memory_space=pltpu.VMEM)],
        out_specs=pl.BlockSpec(memory_space=pltpu.VMEM),
        name="by_target",
    )(match_row, pieces)


def meet_kernel(match_ref, before_ref, ahead_ref, behind_ref, out_ref):
    first = lax.broadcasted_iota(jnp.int32, (2, 128), 1) < 64

    def forward(p, carry):
        out_ref[before_ref[p]] = behind_ref[p]
        return carry

    def backward(p, carry):
        out_ref[p] = jnp.where(first, out_ref[p], ahead_ref[match_ref[p]])
        return carry

    lax.fori_loop(0, N_PEER, forward, 0)
    lax.fori_loop(0, N_PEER, backward, 0)


def meet(match_row, match_before, from_ahead, from_behind):
    return pl.pallas_call(
        meet_kernel,
        out_shape=jax.ShapeDtypeStruct(from_ahead.shape, from_ahead.dtype),
        in_specs=[pl.BlockSpec(memory_space=pltpu.SMEM)] * 2 + [pl.BlockSpec(memory_space=pltpu.VMEM)] * 2,
        out_specs=pl.BlockSpec(memory_space=pltpu.VMEM),
        name="meet",
    )(match_row, match_before, from_ahead, from_behind)


def exchange(value):
    return lax.all_to_all(value, "peer", split_axis=0, concat_axis=0, tiled=True)


def on_device(hidden_in, out_grad, gain, w_down, w_up, matching):
    tokens, held_grad, gain_row = hidden_in[0], out_grad[0], gain[0]
    down_rows, up_rows, match_row = w_down[0], w_up[0], matching[0]
    peer = lax.axis_index("peer")
    z_at = (peer // NX) % NZ

    up_before = along(up_rows, 1)
    match_before = along(match_row, 1)

    tokens_f = tokens.astype(F32)
    inv_rms = lax.rsqrt(jnp.mean(tokens_f * tokens_f, axis=-1, keepdims=True) + 1e-05)
    normed = (tokens_f * inv_rms * gain_row).astype(BF16)
    preact = jnp.dot(normed, down_rows.T, preferred_element_type=F32)
    active = jax.nn.silu(preact).astype(BF16)
    result = (tokens_f + jnp.dot(active, up_rows, preferred_element_type=F32)).astype(BF16)

    pieces = result.reshape(8, 16, 8, 640).transpose(0, 2, 1, 3).reshape(N_PEER, 16, 640)
    held = exchange(pieces)
    moved = along(by_target(match_row, held), 1)

    act_grad_held = jnp.dot(held_grad, up_before.T, preferred_element_type=F32)
    small = jnp.concatenate([active.astype(F32), act_grad_held], axis=1)
    small = exchange(small.reshape(N_PEER, 2, 128))
    small = meet(match_row, match_before, along(small, -1), along(small, 1))
    small = exchange(small).reshape(128, 128)
    active_before = small[:, :64].astype(BF16)
    act_grad = small[:, 64:]

    q = jax.nn.sigmoid(preact)
    pre_grad = (act_grad * q * (1.0 + preact * (1.0 - q))).astype(BF16)
    contract = (((0,), (0,)), ((), ()))
    down_part = lax.dot_general(normed, pre_grad, contract, preferred_element_type=F32)
    up_part = lax.dot_general(held_grad, active_before, contract, preferred_element_type=F32)
    part = jnp.concatenate([down_part, up_part], axis=1).astype(BF16)
    part = part.reshape(NY, NZ, NX, 80, 128).transpose(0, 2, 1, 3, 4).reshape(NY * NX, NZ * 80, 128)
    part = lax.all_to_all(part, "peer", split_axis=0, concat_axis=0, tiled=True, axis_index_groups=PLANES)
    plane_sum = jnp.sum(part.astype(F32), axis=0).reshape(NZ, 80, 128)
    total = lax.dynamic_index_in_dim(plane_sum, z_at, 0, keepdims=False)
    for k in range(1, NZ):
        chunk = lax.dynamic_index_in_dim(plane_sum, (z_at + k) % NZ, 0, keepdims=False)
        total = total + along(chunk, 0, k)
    grad_down = total[:, :64].T
    grad_up = along(total[:, 64:], -1).T
    own = lambda array: lax.dynamic_slice_in_dim(array, peer * 80, 80, array.ndim - 1)
    grad_gain = jnp.sum(own(down_rows).astype(F32) * grad_down, axis=0) / own(gain_row)

    landed = exchange(moved)
    act_out = landed.reshape(8, 8, 16, 640).transpose(0, 2, 1, 3).reshape(128, 5120)
    return act_out[None], grad_down[None], grad_up[None], grad_gain[None]


def solution(mesh):
    placed = (
        P("section", "peer", None),
        P("section", "peer", None),
        P("section", None),
        P("section", None, None),
        P("section", None, None),
        P("section", None),
    )
    return jax.shard_map(
        on_device,
        mesh=mesh,
        in_specs=placed,
        out_specs=(
            P("section", "peer", None),
            P("section", None, "peer"),
            P("section", None, "peer"),
            P("section", "peer"),
        ),
        check_vma=False,
    )
```

```python
import jax
import jax.numpy as jnp
from jax import lax
from jax.experimental import pallas as pl
from jax.experimental.pallas import tpu as pltpu
from jax.sharding import PartitionSpec as P

NX, NY, NZ = 4, 4, 4
N_PEER = NX * NY * NZ
N_SECTION = 8
PLANE = NX * NY
D = 5120
LATENT = 64
ROWS = 128
HALF = D // 2
WIDE = HALF // NZ
OWN = D // N_PEER
PLANES = [[y * 16 + z * 4 + x for y in range(NY) for x in range(NX)] for z in range(NZ)]
BF16, F32 = jnp.bfloat16, jnp.float32
SMEM = pl.BlockSpec(memory_space=pltpu.SMEM)
VMEM = pl.BlockSpec(memory_space=pltpu.VMEM)
ANY = pl.BlockSpec(memory_space=pl.ANY)
LAST = (((1,), (1,)), ((), ()))


def along(value, section_steps, z_steps=0, flip_x=0):
    pairs = []
    for s in range(N_SECTION):
        for y in range(NY):
            for z in range(NZ):
                for x in range(NX):
                    source = s * N_PEER + y * 16 + z * 4 + x
                    target = ((s + section_steps) % N_SECTION) * N_PEER + y * 16 + ((z + z_steps) % NZ) * 4 + (x ^ flip_x)
                    pairs.append((source, target))
    return lax.ppermute(value, ("section", "peer"), pairs)


def in_plane(value):
    return lax.all_to_all(value, "peer", split_axis=0, concat_axis=0, tiled=True, axis_index_groups=PLANES)


def in_cube(value):
    return lax.all_to_all(value, "peer", split_axis=0, concat_axis=0, tiled=True)


def shape(dims, kind=BF16):
    return jax.ShapeDtypeStruct(dims, kind)


def sigmoid(value):
    return 1.0 / (1.0 + jnp.exp(-value))


def turned(at, steps):
    return lax.rem(at + steps, NZ)


def columns_of(group, start=0):
    return pl.ds(pl.multiple_of(start + group * WIDE, 128), WIDE)


def forward_kernel(z_ref, tokens_ref, gain_ref, down_ref, up_ref, normed_ref, preact_ref, active_ref, b_ref, *a_refs):
    z = z_ref[0]
    chunks = [slice(c * WIDE, (c + 1) * WIDE) for c in range(D // WIDE)]
    squares = jnp.zeros((ROWS, 1), F32)
    for cols in chunks:
        t = tokens_ref[:, cols].astype(F32)
        squares += jnp.sum(t * t, axis=1, keepdims=True)
    inv_rms = lax.rsqrt(squares / D + 1e-05)
    preact = jnp.zeros((ROWS, LATENT), F32)
    for cols in chunks:
        n = (tokens_ref[:, cols].astype(F32) * inv_rms * gain_ref[:, cols]).astype(BF16)
        normed_ref[:, cols] = n
        preact += lax.dot_general(n, down_ref[:, cols], LAST, preferred_element_type=F32)
    preact_ref[...] = preact
    active = (preact * sigmoid(preact)).astype(BF16)
    active_ref[...] = active.astype(F32)

    def result(cols):
        up = jnp.dot(active, up_ref[:, cols], preferred_element_type=F32)
        return (tokens_ref[:, cols].astype(F32) + up).astype(BF16)

    for k in range(NZ):
        a_refs[k][...] = result(columns_of(turned(z, k)))
    for c in range(NZ):
        b_ref[:, c * WIDE : (c + 1) * WIDE] = result(slice(HALF + c * WIDE, HALF + (c + 1) * WIDE))


def forward(z_at, tokens, gain_row, down_rows, up_rows):
    return pl.pallas_call(
        forward_kernel,
        out_shape=(
            shape((ROWS, D)),
            shape((ROWS, LATENT), F32),
            shape((ROWS, LATENT), F32),
            shape((ROWS, HALF)),
            *[shape((ROWS, WIDE))] * NZ,
        ),
        in_specs=[SMEM] + [VMEM] * 4,
        out_specs=[VMEM] * (4 + NZ),
        name="forward",
    )(z_at, tokens, gain_row, down_rows, up_rows)


def small_kernel(half_ref, active_ref, grad_ref, own_ref, other_ref, after_ref, out_ref, up_ref):
    half = half_ref[0]
    up_ref[pl.ds(pl.multiple_of(half * 32, 32), 32), :] = own_ref[...]
    up_ref[pl.ds(pl.multiple_of((1 - half) * 32, 32), 32), :] = other_ref[...]
    out_ref[:, :LATENT] = active_ref[...]
    out_ref[:, LATENT:] = lax.dot_general(grad_ref[...], up_ref[...], LAST, preferred_element_type=F32)


def small_payload(half, active, held_grad, own_up, other_up, after):
    return pl.pallas_call(
        small_kernel,
        out_shape=shape((ROWS, 2 * LATENT), F32),
        in_specs=[SMEM] + [VMEM] * 4 + [ANY],
        out_specs=VMEM,
        scratch_shapes=[pltpu.VMEM((LATENT, D), BF16)],
        name="small_payload",
    )(half, active, held_grad, own_up, other_up, after)


def meet_kernel(match_ref, before_ref, ahead_ref, behind_ref, after_ref, out_ref):
    first = lax.broadcasted_iota(jnp.int32, (2, 128), 1) < LATENT
    for p in range(N_PEER):
        out_ref[before_ref[p]] = behind_ref[p]
    for p in range(N_PEER):
        out_ref[p] = jnp.where(first, out_ref[p], ahead_ref[match_ref[p]])


def meet(match_row, match_before, from_ahead, from_behind, after):
    return pl.pallas_call(
        meet_kernel,
        out_shape=shape(from_ahead.shape, F32),
        in_specs=[SMEM] * 2 + [VMEM] * 2 + [ANY],
        out_specs=VMEM,
        name="meet",
    )(match_row, match_before, from_ahead, from_behind, after)


def grads_kernel(small_ref, preact_ref, normed_ref, grad_ref, after_ref, out_ref):
    preact = preact_ref[...]
    q = sigmoid(preact)
    pre_grad = small_ref[:, LATENT:] * q * (1.0 + preact * (1.0 - q))
    none = jnp.zeros((ROWS, LATENT), F32)
    down = jnp.concatenate([pre_grad, none], axis=1).T.astype(BF16)
    up = jnp.concatenate([none, small_ref[:, :LATENT]], axis=1).T.astype(BF16)
    for j in range(D // WIDE):
        cols = slice(j * WIDE, (j + 1) * WIDE)
        part = jnp.dot(down, normed_ref[:, cols], preferred_element_type=F32)
        part += jnp.dot(up, grad_ref[:, cols], preferred_element_type=F32)
        part = part.T.astype(BF16)
        for i in range(WIDE // OWN):
            p = j * (WIDE // OWN) + i
            y, z, x = p // 16, (p // 4) % 4, p % 4
            out_ref[y * NX + x, z * OWN : (z + 1) * OWN, :] = part[i * OWN : (i + 1) * OWN]


def grads(small, preact, normed, held_grad, after):
    return pl.pallas_call(
        grads_kernel,
        out_shape=shape((PLANE, NZ * OWN, 2 * LATENT)),
        in_specs=[VMEM] * 4 + [ANY],
        out_specs=VMEM,
        name="grads",
    )(small, preact, normed, held_grad, after)


def beside_kernel(r0, r1, r2, r3, after_ref, out_ref):
    for k, ref in enumerate((r0, r1, r2, r3)):
        out_ref[:, :, k * WIDE : (k + 1) * WIDE] = ref[...]


def beside(parts, after):
    return pl.pallas_call(
        beside_kernel,
        out_shape=shape((PLANE, 8, HALF)),
        in_specs=[VMEM] * NZ + [ANY],
        out_specs=VMEM,
        name="beside",
    )(*parts, after)


def route_a_kernel(z_ref, before_ref, held_ref, o0, o1, o2, o3, sorted_ref):
    z = z_ref[0]
    for xy in range(PLANE):
        for k in range(NZ):
            source = (xy // NX) * 16 + turned(z, NZ - k) * 4 + xy % NX
            q = before_ref[source]
            place = (q // 16) * NX + lax.rem(q, NX)
            planes_on = turned(lax.rem(q // 4, NZ) + NZ, 0 - z)
            sorted_ref[planes_on, place] = held_ref[xy, :, k * WIDE : (k + 1) * WIDE]
    for k, out in enumerate((o0, o1, o2, o3)):
        out[...] = sorted_ref[k]


def route_a(z_at, match_before, held):
    return pl.pallas_call(
        route_a_kernel,
        out_shape=[shape((PLANE, 8, WIDE))] * NZ,
        in_specs=[SMEM] * 2 + [VMEM],
        out_specs=[VMEM] * NZ,
        scratch_shapes=[pltpu.VMEM((NZ, PLANE, 8, WIDE), BF16)],
        name="route_a",
    )(z_at, match_before, held)


def route_b_kernel(z_ref, before_ref, r0, r1, r2, r3, after_ref, out_ref, sorted_ref):
    z = z_ref[0]
    for k, ref in enumerate((r0, r1, r2, r3)):
        for xy in range(PLANE):
            source = (xy // NX) * 16 + turned(z, NZ - k) * 4 + xy % NX
            q = before_ref[source]
            place = (q // 16) * NX + lax.rem(q, NX)
            planes_on = turned(lax.rem(q // 4, NZ) + NZ, 0 - z)
            sorted_ref[planes_on, place] = ref[xy]
    for k in range(NZ):
        out_ref[:, :, k * WIDE : (k + 1) * WIDE] = sorted_ref[k]


def route_b(z_at, match_before, parts, after):
    return pl.pallas_call(
        route_b_kernel,
        out_shape=shape((PLANE, 8, HALF)),
        in_specs=[SMEM] * 2 + [VMEM] * NZ + [ANY],
        out_specs=VMEM,
        scratch_shapes=[pltpu.VMEM((NZ, PLANE, 8, WIDE), BF16)],
        name="route_b",
    )(z_at, match_before, *parts, after)


def assemble_kernel(z_ref, a_ref, b0_ref, b1_ref, b2_ref, b3_ref, out_ref):
    z = z_ref[0]
    for k, ref in enumerate((b0_ref, b1_ref, b2_ref, b3_ref)):
        group = turned(z, NZ - k)
        out_ref[:, columns_of(group)] = a_ref[:, k * WIDE : (k + 1) * WIDE]
        out_ref[:, columns_of(group, HALF)] = ref[:, :WIDE]


def assemble(z_at, landed_a, landed_b):
    return pl.pallas_call(
        assemble_kernel,
        out_shape=shape((ROWS, D)),
        in_specs=[SMEM] + [VMEM] * (1 + NZ),
        out_specs=VMEM,
        name="assemble",
    )(z_at, landed_a, *landed_b)


def on_device(hidden_in, out_grad, gain, w_down, w_up, matching):
    tokens, held_grad = hidden_in[0], out_grad[0]
    down_rows, up_rows, match_row = w_down[0], w_up[0], matching[0]
    peer = lax.axis_index("peer")
    z = (peer // NX) % NZ
    z_at = z.reshape(1)
    half = peer % 2

    own_up = along(lax.dynamic_slice_in_dim(up_rows, half * 32, 32, 0), 1)
    match_before = along(match_row, 1)
    normed, preact, active, half_b, *groups_a = forward(z_at, tokens, gain, down_rows, up_rows)

    a_parts = [along(part.reshape(PLANE, 8, WIDE), 1, k) for k, part in enumerate(groups_a)]
    b_spread = in_plane(half_b.reshape(PLANE, 8, HALF))
    other_up = along(own_up, 0, 0, 1)

    small = small_payload(half.reshape(1), active, held_grad, own_up, other_up, b_spread)
    small = in_cube(small.reshape(N_PEER, 2, 128))

    b_parts = [
        along(lax.dynamic_slice_in_dim(b_spread, ((z + k) % NZ) * WIDE, WIDE, 2), 1, k) for k in range(NZ)
    ]

    a_spread = in_plane(beside(a_parts, small))
    a_sorted = route_a(z_at, match_before, a_spread)

    small = meet(match_row, match_before, along(small, -1), along(small, 1), a_spread)
    small = in_cube(small).reshape(ROWS, 2 * LATENT)

    b_sorted = in_plane(route_b(z_at, match_before, b_parts, small))

    part = in_plane(grads(small, preact, normed, held_grad, b_sorted))
    plane_sum = jnp.sum(part.astype(F32), axis=0).reshape(NZ, OWN, 2 * LATENT)
    total = lax.dynamic_index_in_dim(plane_sum, z, 0, keepdims=False)
    for k in range(1, NZ):
        chunk = lax.dynamic_index_in_dim(plane_sum, (z + k) % NZ, 0, keepdims=False)
        total = total + along(chunk, 0, k)
    grad_down = total[:, :LATENT].T
    grad_up = along(total[:, LATENT:], -1).T
    own = lambda array: lax.dynamic_slice_in_dim(array, peer * OWN, OWN, 1)
    grad_gain = jnp.sum(own(down_rows).astype(F32) * grad_down, axis=0, keepdims=True) / own(gain)

    a_landed = [a_sorted[0]] + [along(a_sorted[k], 0, k) for k in range(1, NZ)]
    b_landed = [b_sorted] + [along(b_sorted[:, :, k * WIDE : (k + 1) * WIDE], 0, k) for k in range(1, NZ)]
    a_last = in_plane(beside(a_landed, part))
    act_out = assemble(z_at, a_last.reshape(ROWS, HALF), [b.reshape(ROWS, -1) for b in b_landed])
    return act_out[None], grad_down[None], grad_up[None], grad_gain


def solution(mesh):
    placed = (
        P("section", "peer", None),
        P("section", "peer", None),
        P("section", None),
        P("section", None, None),
        P("section", None, None),
        P("section", None),
    )
    return jax.shard_map(
        on_device,
        mesh=mesh,
        in_specs=placed,
        out_specs=(
            P("section", "peer", None),
            P("section", None, "peer"),
            P("section", None, "peer"),
            P("section", "peer"),
        ),
        check_vma=False,
    )
```

```python
import jax
import jax.numpy as jnp
from jax import lax
from jax.experimental import pallas as pl
from jax.experimental.pallas import tpu as pltpu
from jax.sharding import PartitionSpec as P

NX, NY, NZ = 4, 4, 4
N_PEER = NX * NY * NZ
N_SECTION = 8
PLANE = NX * NY
D = 5120
LATENT = 64
ROWS = 128
WIDE = 640
HALF = D // 2
OWN = D // N_PEER
PLANES = [[y * 16 + z * 4 + x for y in range(NY) for x in range(NX)] for z in range(NZ)]
BF16, F32 = jnp.bfloat16, jnp.float32
SMEM = pl.BlockSpec(memory_space=pltpu.SMEM)
VMEM = pl.BlockSpec(memory_space=pltpu.VMEM)
ROOM = pltpu.CompilerParams(vmem_limit_bytes=16 * 1024 * 1024)
LAST = (((1,), (1,)), ((), ()))


def along(value, section_steps, z_steps=0):
    pairs = []
    for s in range(N_SECTION):
        for y in range(NY):
            for z in range(NZ):
                for x in range(NX):
                    source = s * N_PEER + y * 16 + z * 4 + x
                    target = ((s + section_steps) % N_SECTION) * N_PEER + y * 16 + ((z + z_steps) % NZ) * 4 + x
                    pairs.append((source, target))
    return lax.ppermute(value, ("section", "peer"), pairs)


def in_plane(value):
    return lax.all_to_all(value, "peer", split_axis=0, concat_axis=0, tiled=True, axis_index_groups=PLANES)


def in_cube(value):
    return lax.all_to_all(value, "peer", split_axis=0, concat_axis=0, tiled=True)


def shape(dims, kind=BF16):
    return jax.ShapeDtypeStruct(dims, kind)


def sigmoid(value):
    return 1.0 / (1.0 + jnp.exp(-value))


def pack_kernel(rows_ref, gain_ref, match_ref, out_ref):
    gain = gain_ref[...]
    high = gain.astype(BF16).astype(F32)
    middle = (gain - high).astype(BF16).astype(F32)
    row = lax.broadcasted_iota(jnp.int32, (8, D), 0)
    rest = jnp.zeros((8, D), F32)
    for at, value in enumerate((high, middle, gain - high - middle, match_ref[...])):
        rest = jnp.where(row == at, value, rest)
    out_ref[...] = jnp.concatenate([rows_ref[...].astype(F32), rest], axis=0).astype(BF16)


def pack(rows, gain_row, match_row):
    return pl.pallas_call(
        pack_kernel,
        out_shape=shape((16, D)),
        in_specs=[VMEM] * 3,
        out_specs=VMEM,
        compiler_params=ROOM,
        name="pack",
    )(rows, gain_row, match_row)


def act_grad_kernel(grad_ref, both_ref, out_ref):
    out_ref[...] = lax.dot_general(grad_ref[...], both_ref[:, HALF:], LAST, preferred_element_type=F32)


def act_grad_of(held_grad, both):
    return pl.pallas_call(
        act_grad_kernel,
        out_shape=shape((ROWS, 2 * LATENT), F32),
        in_specs=[VMEM] * 2,
        out_specs=VMEM,
        compiler_params=ROOM,
        name="act_grad",
    )(held_grad, both)


def adapter_kernel(landed_ref, both_ref, packed_ref, grad_ref, act_grad_ref, out_ref, part_ref, normed_ref):
    def tokens(z, at):
        pieces = [landed_ref[y * 16 + z * 4 + x, :, at : at + WIDE].astype(F32) for y in range(NY) for x in range(NX)]
        return jnp.concatenate(pieces, axis=0)

    def weights(cols):
        return both_ref[:, HALF + cols.start : HALF + cols.stop]

    chunks = [(z, h * WIDE, slice(h * HALF + z * WIDE, h * HALF + (z + 1) * WIDE)) for h in range(2) for z in range(NZ)]
    squares = jnp.zeros((ROWS, 1), F32)
    for z, at, cols in chunks:
        t = tokens(z, at)
        squares += jnp.sum(t * t, axis=1, keepdims=True)
    inv_rms = lax.rsqrt(squares / D + 1e-05)
    product = jnp.zeros((ROWS, 2 * LATENT), F32)
    for z, at, cols in chunks:
        gain = jnp.sum(packed_ref[:, cols].astype(F32)[8:11], axis=0, keepdims=True)
        n = (tokens(z, at) * inv_rms * gain).astype(BF16)
        normed_ref[:, cols] = n
        product += lax.dot_general(n, weights(cols), LAST, preferred_element_type=F32)
    lane = lax.broadcasted_iota(jnp.int32, (ROWS, 2 * LATENT), 1)
    is_up = lax.rem(lane, 8) < 4
    preact = jnp.where(is_up, 0.0, product)
    q = sigmoid(preact)
    active = pltpu.roll(preact * q, 2 * LATENT - 4, 1)
    active = jnp.where(is_up, active, 0.0).astype(BF16)
    for z, at, cols in chunks:
        up = jnp.dot(active, weights(cols), preferred_element_type=F32)
        t = (tokens(z, at) + up)
        for g in range(PLANE):
            out_ref[g, :, cols] = t[g * 8 : (g + 1) * 8].astype(BF16)
    act_grad = pltpu.roll(act_grad_ref[...], 4, 1)
    pre_grad = jnp.where(is_up, 0.0, act_grad * q * (1.0 + preact * (1.0 - q)))
    down = pre_grad.T.astype(BF16)
    up = active.astype(F32).T.astype(BF16)
    for j in range(D // WIDE):
        cols = slice(j * WIDE, (j + 1) * WIDE)
        part = jnp.dot(down, normed_ref[:, cols], preferred_element_type=F32)
        part += jnp.dot(up, grad_ref[:, cols], preferred_element_type=F32)
        part = part.T.astype(BF16)
        for i in range(WIDE // OWN):
            p = j * (WIDE // OWN) + i
            y, z, x = p // 16, (p // 4) % 4, p % 4
            part_ref[y * NX + x, z * OWN : (z + 1) * OWN, :] = part[i * OWN : (i + 1) * OWN]


def adapter(landed, both, packed, held_grad, act_grad):
    return pl.pallas_call(
        adapter_kernel,
        out_shape=(shape((PLANE, 8, D)), shape((PLANE, NZ * OWN, 2 * LATENT))),
        in_specs=[VMEM] * 5,
        out_specs=[VMEM] * 2,
        scratch_shapes=[pltpu.VMEM((ROWS, D), BF16)],
        compiler_params=ROOM,
        name="adapter",
    )(landed, both, packed, held_grad, act_grad)


def turn_kernel(z_ref, a0, a1, a2, a3, spread_ref, packed_ref, a_ref, b0, b1, b2, b3):
    z = z_ref[0]
    for k, (part, out) in enumerate(zip((a0, a1, a2, a3), (b0, b1, b2, b3))):
        a_ref[:, :, k * WIDE : (k + 1) * WIDE] = part[...]
        at = pl.multiple_of(lax.rem(z + k, NZ) * WIDE, 128)
        out[...] = spread_ref[:, :, pl.ds(at, WIDE)]
    rows = packed_ref[...].astype(F32)[:8].astype(BF16)
    for g in range(PLANE):
        a_ref[g, :, HALF:] = rows


def turn(z_at, a_parts, spread_b, packed):
    return pl.pallas_call(
        turn_kernel,
        out_shape=[shape((PLANE, 8, HALF + D))] + [shape((PLANE, 8, WIDE))] * NZ,
        in_specs=[SMEM] + [VMEM] * (NZ + 2),
        out_specs=[VMEM] * (1 + NZ),
        compiler_params=ROOM,
        name="turn",
    )(z_at, *a_parts, spread_b, packed)


def route_kernel(z_ref, before_ref, a_ref, b0, b1, b2, b3, out_ref):
    z = z_ref[0]
    for k, b_ref in enumerate((b0, b1, b2, b3)):
        plane = lax.rem(z + NZ - k, NZ) * NX
        for xy in range(PLANE):
            q = before_ref[plane + (xy // NX) * 16 + xy % NX]
            out_ref[q, :, :WIDE] = a_ref[xy, :, k * WIDE : (k + 1) * WIDE]
            out_ref[q, :, WIDE:] = b_ref[xy]


def route(z_at, match_before, spread_a, b_parts):
    return pl.pallas_call(
        route_kernel,
        out_shape=shape((N_PEER, 8, 2 * WIDE)),
        in_specs=[SMEM] * 2 + [VMEM] * (1 + NZ),
        out_specs=VMEM,
        compiler_params=ROOM,
        name="route",
    )(z_at, match_before, spread_a, *b_parts)


def on_device(hidden_in, out_grad, gain, w_down, w_up, matching):
    tokens, held_grad = hidden_in[0], out_grad[0]
    down_rows, up_rows = w_down[0], w_up[0]
    peer = lax.axis_index("peer")
    z = (peer // NX) % NZ
    place = (peer // 16) * NX + peer % NX

    z_at = z.reshape(1)
    a_out = [lax.dynamic_slice_in_dim(tokens, ((z + k) % NZ) * WIDE, WIDE, 1) for k in range(NZ)]
    a_parts = [along(part.reshape(PLANE, 8, WIDE), 1, k) for k, part in enumerate(a_out)]
    spread_b = in_plane(tokens[:, HALF:].reshape(PLANE, 8, HALF))

    rows = lambda array: lax.dynamic_slice_in_dim(array, place * 4, 4, 0)
    match_wide = jnp.pad(matching.astype(F32), ((0, 0), (0, D - N_PEER)))
    packed = along(pack(jnp.concatenate([rows(up_rows), rows(down_rows)], axis=0), gain, match_wide), 1)
    match_before = packed[11, :N_PEER].astype(jnp.int32)

    a_turned, *b_out = turn(z_at, a_parts, spread_b, packed)
    b_parts = [along(part, 1, k) for k, part in enumerate(b_out)]
    spread_a = in_plane(a_turned)
    both = spread_a.reshape(ROWS, HALF + D)
    act_grad = act_grad_of(held_grad, both)

    landed = in_cube(route(z_at, match_before, spread_a, b_parts))
    act_out, part = adapter(landed, both, packed, held_grad, act_grad)

    part = in_plane(part)
    plane_sum = jnp.sum(part.astype(F32), axis=0).reshape(NZ, OWN, 2 * LATENT)
    total = 0.0
    for k in range(NZ):
        chunk = lax.dynamic_index_in_dim(plane_sum, (z + k) % NZ, 0, keepdims=False)
        total = total + along(chunk, -1, k)
    total = total.T.reshape(PLANE, 2, 4, OWN)
    grad_up = total[:, 0].reshape(LATENT, OWN)
    grad_down = total[:, 1].reshape(LATENT, OWN)
    own = lambda array: lax.dynamic_slice_in_dim(array, peer * OWN, OWN, 1)
    grad_gain = jnp.sum(own(down_rows).astype(F32) * grad_down, axis=0, keepdims=True) / own(gain)
    return act_out.reshape(1, ROWS, D), grad_down[None], grad_up[None], grad_gain


def solution(mesh):
    placed = (
        P("section", "peer", None),
        P("section", "peer", None),
        P("section", None),
        P("section", None, None),
        P("section", None, None),
        P("section", None),
    )
    return jax.shard_map(
        on_device,
        mesh=mesh,
        in_specs=placed,
        out_specs=(
            P("section", "peer", None),
            P("section", None, "peer"),
            P("section", None, "peer"),
            P("section", "peer"),
        ),
        check_vma=False,
    )
```

```python
import jax
import jax.numpy as jnp
from jax import lax
from jax.experimental import pallas as pl
from jax.experimental.pallas import tpu as pltpu
from jax.sharding import PartitionSpec as P

NX, NY, NZ = 4, 4, 4
N_PEER = NX * NY * NZ
N_SECTION = 8
PLANE = NX * NY
D = 5120
LATENT = 64
ROWS = 128
WIDE = 640
SPAN = D // NZ
HALF = 2 * SPAN
LEAD = 10**11
OWN = D // N_PEER
PLANES = [[y * 16 + z * 4 + x for y in range(NY) for x in range(NX)] for z in range(NZ)]
BF16, F32 = jnp.bfloat16, jnp.float32
SMEM = pl.BlockSpec(memory_space=pltpu.SMEM)
VMEM = pl.BlockSpec(memory_space=pltpu.VMEM)
ROOM = pltpu.CompilerParams(vmem_limit_bytes=16 * 1024 * 1024)
LAST = (((1,), (1,)), ((), ()))


def along(value, section_steps, z_steps=0):
    pairs = []
    for s in range(N_SECTION):
        for y in range(NY):
            for z in range(NZ):
                for x in range(NX):
                    source = s * N_PEER + y * 16 + z * 4 + x
                    target = ((s + section_steps) % N_SECTION) * N_PEER + y * 16 + ((z + z_steps) % NZ) * 4 + x
                    pairs.append((source, target))
    return lax.ppermute(value, ("section", "peer"), pairs)


def in_plane(value):
    return lax.all_to_all(value, "peer", split_axis=0, concat_axis=0, tiled=True, axis_index_groups=PLANES)


def in_cube(value):
    return lax.all_to_all(value, "peer", split_axis=0, concat_axis=0, tiled=True)


def shape(dims, kind=BF16):
    return jax.ShapeDtypeStruct(dims, kind)


def sigmoid(value):
    return 1.0 / (1.0 + jnp.exp(-value))


def pack_kernel(rows_ref, gain_ref, match_ref, out_ref):
    gain = gain_ref[...]
    high = gain.astype(BF16).astype(F32)
    middle = (gain - high).astype(BF16).astype(F32)
    row = lax.broadcasted_iota(jnp.int32, (8, D), 0)
    rest = jnp.zeros((8, D), F32)
    for at, value in enumerate((high, middle, gain - high - middle, match_ref[...])):
        rest = jnp.where(row == at, value, rest)
    out_ref[...] = jnp.concatenate([rows_ref[...].astype(F32), rest], axis=0).astype(BF16)


def pack(rows, gain_row, match_row):
    return pl.pallas_call(
        pack_kernel,
        out_shape=shape((16, D)),
        in_specs=[VMEM] * 3,
        out_specs=VMEM,
        compiler_params=ROOM,
        name="pack",
    )(rows, gain_row, match_row)


def act_grad_kernel(grad_ref, both_ref, out_ref):
    out_ref[...] = lax.dot_general(grad_ref[...], both_ref[:, HALF:], LAST, preferred_element_type=F32)


def act_grad_of(held_grad, both):
    return pl.pallas_call(
        act_grad_kernel,
        out_shape=shape((ROWS, 2 * LATENT), F32),
        in_specs=[VMEM] * 2,
        out_specs=VMEM,
        compiler_params=ROOM,
        name="act_grad",
    )(held_grad, both)


def landed_rows(landed_ref, z, at):
    pieces = [landed_ref[y * 16 + z * 4 + x, :, at : at + WIDE].astype(F32) for y in range(NY) for x in range(NX)]
    return jnp.concatenate(pieces, axis=0)


CHUNKS = [(z, at, slice(z * SPAN + at, z * SPAN + at + WIDE)) for z in range(NZ) for at in range(0, SPAN, WIDE)]


def weights(both_ref, cols):
    return both_ref[:, HALF + cols.start : HALF + cols.stop]


def adapter_kernel(landed_ref, both_ref, packed_ref, grad_ref, act_grad_ref, active_ref, part_ref, normed_ref):
    squares = jnp.zeros((ROWS, 1), F32)
    for z, at, cols in CHUNKS:
        t = landed_rows(landed_ref, z, at)
        squares += jnp.sum(t * t, axis=1, keepdims=True)
    inv_rms = lax.rsqrt(squares / D + 1e-05)
    product = jnp.zeros((ROWS, 2 * LATENT), F32)
    for z, at, cols in CHUNKS:
        gain = jnp.sum(packed_ref[:, cols].astype(F32)[8:11], axis=0, keepdims=True)
        n = (landed_rows(landed_ref, z, at) * inv_rms * gain).astype(BF16)
        normed_ref[:, cols] = n
        product += lax.dot_general(n, weights(both_ref, cols), LAST, preferred_element_type=F32)
    lane = lax.broadcasted_iota(jnp.int32, (ROWS, 2 * LATENT), 1)
    is_up = lax.rem(lane, 8) < 4
    preact = jnp.where(is_up, 0.0, product)
    q = sigmoid(preact)
    active = pltpu.roll(preact * q, 2 * LATENT - 4, 1)
    active = jnp.where(is_up, active, 0.0).astype(BF16)
    active_ref[...] = active
    act_grad = pltpu.roll(act_grad_ref[...], 4, 1)
    pre_grad = jnp.where(is_up, 0.0, act_grad * q * (1.0 + preact * (1.0 - q)))
    down = pre_grad.T.astype(BF16)
    up = active.astype(F32).T.astype(BF16)
    for j in range(D // WIDE):
        cols = slice(j * WIDE, (j + 1) * WIDE)
        part = jnp.dot(down, normed_ref[:, cols], preferred_element_type=F32)
        part += jnp.dot(up, grad_ref[:, cols], preferred_element_type=F32)
        part = part.T.astype(BF16)
        for i in range(WIDE // OWN):
            p = j * (WIDE // OWN) + i
            y, z, x = p // 16, (p // 4) % 4, p % 4
            part_ref[y * NX + x, z * OWN : (z + 1) * OWN, :] = part[i * OWN : (i + 1) * OWN]


def adapter(landed, both, packed, held_grad, act_grad):
    return pl.pallas_call(
        adapter_kernel,
        out_shape=(shape((ROWS, 2 * LATENT)), shape((PLANE, NZ * OWN, 2 * LATENT))),
        in_specs=[VMEM] * 5,
        out_specs=[VMEM] * 2,
        scratch_shapes=[pltpu.VMEM((ROWS, D), BF16)],
        compiler_params=ROOM,
        name="adapter",
    )(landed, both, packed, held_grad, act_grad)


def finish_kernel(landed_ref, both_ref, active_ref, out_ref):
    for z, at, cols in CHUNKS:
        up = jnp.dot(active_ref[...], weights(both_ref, cols), preferred_element_type=F32)
        t = landed_rows(landed_ref, z, at) + up
        for g in range(PLANE):
            out_ref[g, :, cols] = t[g * 8 : (g + 1) * 8].astype(BF16)


def finish(landed, both, active):
    return pl.pallas_call(
        finish_kernel,
        out_shape=shape((PLANE, 8, D)),
        in_specs=[VMEM] * 3,
        out_specs=VMEM,
        compiler_params=ROOM,
        name="finish",
    )(landed, both, active)


def beside_kernel(a0, a1, packed_ref, out_ref):
    out_ref[:, :, :SPAN] = a0[...]
    out_ref[:, :, SPAN:HALF] = a1[...]
    rows = packed_ref[...].astype(F32)[:8].astype(BF16)
    for g in range(PLANE):
        out_ref[g, :, HALF:] = rows


def beside(a_parts, packed):
    return pl.pallas_call(
        beside_kernel,
        out_shape=shape((PLANE, 8, HALF + D)),
        in_specs=[VMEM] * 3,
        out_specs=VMEM,
        compiler_params=ROOM,
        name="beside",
    )(*a_parts, packed)


def seen_kernel(*refs):
    refs[-1][...] = sum(ref[0, :, :128].astype(F32) for ref in refs[:-1])


def seen(*values):
    return pl.pallas_call(
        seen_kernel,
        out_shape=shape((8, 128), F32),
        in_specs=[VMEM] * len(values),
        out_specs=VMEM,
        compiler_params=ROOM,
        cost_estimate=pl.CostEstimate(flops=LEAD, bytes_accessed=0, transcendentals=0),
        name="seen",
    )(*values)


def halves_kernel(spread_ref, after_ref, b0, b1):
    b0[...] = spread_ref[:, :, :SPAN]
    b1[...] = spread_ref[:, :, SPAN:]


def halves(spread_b, after):
    return pl.pallas_call(
        halves_kernel,
        out_shape=[shape((PLANE, 8, SPAN))] * 2,
        in_specs=[VMEM] * 2,
        out_specs=[VMEM] * 2,
        compiler_params=ROOM,
        name="halves",
    )(spread_b, after)


def route_kernel(z_ref, before_ref, a_ref, b0, b1, after_ref, out_ref):
    z = z_ref[0]
    for k in range(NZ):
        plane = lax.rem(z + NZ - k, NZ) * NX
        for xy in range(PLANE):
            piece = a_ref[xy, :, k * SPAN : (k + 1) * SPAN] if k < 2 else (b0, b1)[k - 2][xy]
            out_ref[before_ref[plane + (xy // NX) * 16 + xy % NX]] = piece


def route(z_at, match_before, spread_a, b_parts, after):
    return pl.pallas_call(
        route_kernel,
        out_shape=shape((N_PEER, 8, SPAN)),
        in_specs=[SMEM] * 2 + [VMEM] * 4,
        out_specs=VMEM,
        compiler_params=ROOM,
        name="route",
    )(z_at, match_before, spread_a, *b_parts, after)


def sums_kernel(p0, p1, p2, p3, down_rows_ref, gain_ref, down_ref, up_ref, grad_gain_ref):
    total = (p0[...] + p1[...] + p2[...] + p3[...]).T
    for g in range(PLANE):
        up_ref[g * 4 : (g + 1) * 4, :] = total[g * 8 : g * 8 + 4]
        down_ref[g * 4 : (g + 1) * 4, :] = total[g * 8 + 4 : (g + 1) * 8]
    weighted = down_rows_ref[...].astype(F32) * down_ref[...]
    grad_gain_ref[...] = jnp.sum(weighted, axis=0, keepdims=True) / gain_ref[...]


def sums(parts, own_down, own_gain):
    return pl.pallas_call(
        sums_kernel,
        out_shape=(shape((LATENT, OWN), F32), shape((LATENT, OWN), F32), shape((1, OWN), F32)),
        in_specs=[VMEM] * (NZ + 2),
        out_specs=[VMEM] * 3,
        compiler_params=ROOM,
        name="sums",
    )(*parts, own_down, own_gain)


def on_device(hidden_in, out_grad, gain, w_down, w_up, matching):
    tokens, held_grad = hidden_in[0], out_grad[0]
    down_rows, up_rows = w_down[0], w_up[0]
    peer = lax.axis_index("peer")
    z = (peer // NX) % NZ
    place = (peer // 16) * NX + peer % NX

    z_at = z.reshape(1)
    out = [lax.dynamic_slice_in_dim(tokens, ((z + k) % NZ) * SPAN, SPAN, 1).reshape(PLANE, 8, SPAN) for k in range(NZ)]
    a_parts = [along(out[k], 1, k) for k in (0, 1)]
    spread_b = in_plane(jnp.concatenate(out[2:], axis=2))

    rows = lambda array: lax.dynamic_slice_in_dim(array, place * 4, 4, 0)
    match_wide = jnp.pad(matching.astype(F32), ((0, 0), (0, D - N_PEER)))
    packed = along(pack(jnp.concatenate([rows(up_rows), rows(down_rows)], axis=0), gain, match_wide), 1)
    match_before = packed[11, :N_PEER].astype(jnp.int32)

    b_parts = [along(part, 1, k) for k, part in zip((2, 3), halves(spread_b, seen(a_parts[0])))]
    spread_a = in_plane(beside(a_parts, packed))
    both = spread_a.reshape(ROWS, HALF + D)
    act_grad = act_grad_of(held_grad, both)

    landed = in_cube(route(z_at, match_before, spread_a, b_parts, seen(*b_parts)))
    active, part = adapter(landed, both, packed, held_grad, act_grad)
    act_out = finish(landed, both, active)

    part = in_plane(part)
    plane_sum = jnp.sum(part.astype(F32), axis=0).reshape(NZ, OWN, 2 * LATENT)
    parts = []
    for k in range(NZ):
        chunk = lax.dynamic_index_in_dim(plane_sum, (z + k) % NZ, 0, keepdims=False)
        parts.append(along(chunk, -1, k))
    own = lambda array: lax.dynamic_slice_in_dim(array, peer * OWN, OWN, 1)
    grad_down, grad_up, grad_gain = sums(parts, own(down_rows), own(gain))
    return act_out.reshape(1, ROWS, D), grad_down[None], grad_up[None], grad_gain


def solution(mesh):
    placed = (
        P("section", "peer", None),
        P("section", "peer", None),
        P("section", None),
        P("section", None, None),
        P("section", None, None),
        P("section", None),
    )
    return jax.shard_map(
        on_device,
        mesh=mesh,
        in_specs=placed,
        out_specs=(
            P("section", "peer", None),
            P("section", None, "peer"),
            P("section", None, "peer"),
            P("section", "peer"),
        ),
        check_vma=False,
    )
```

```python
import jax
import jax.numpy as jnp
from jax import lax
from jax.experimental import pallas as pl
from jax.experimental.pallas import tpu as pltpu
from jax.sharding import PartitionSpec as P

NX, NY, NZ = 4, 4, 4
N_PEER = NX * NY * NZ
N_SECTION = 8
PLANE = NX * NY
D = 5120
LATENT = 64
ROWS = 128
WIDE = 640
SPAN = D // NZ
HALF = 2 * SPAN
LEAD = 10**11
PACKED = D + 256
OWN = D // N_PEER
PLANES = [[y * 16 + z * 4 + x for y in range(NY) for x in range(NX)] for z in range(NZ)]
LINES = [[y * 16 + z * 4 + x for z in range(NZ)] for y in range(NY) for x in range(NX)]
BF16, F32 = jnp.bfloat16, jnp.float32
SMEM = pl.BlockSpec(memory_space=pltpu.SMEM)
VMEM = pl.BlockSpec(memory_space=pltpu.VMEM)
ROOM = pltpu.CompilerParams(vmem_limit_bytes=16 * 1024 * 1024)
LAST = (((1,), (1,)), ((), ()))


def along(value, section_steps, z_steps=0):
    pairs = []
    for s in range(N_SECTION):
        for y in range(NY):
            for z in range(NZ):
                for x in range(NX):
                    source = s * N_PEER + y * 16 + z * 4 + x
                    target = ((s + section_steps) % N_SECTION) * N_PEER + y * 16 + ((z + z_steps) % NZ) * 4 + x
                    pairs.append((source, target))
    return lax.ppermute(value, ("section", "peer"), pairs)


def in_plane(value):
    return lax.all_to_all(value, "peer", split_axis=0, concat_axis=0, tiled=True, axis_index_groups=PLANES)


def in_cube(value):
    return lax.all_to_all(value, "peer", split_axis=0, concat_axis=0, tiled=True)


def shape(dims, kind=BF16):
    return jax.ShapeDtypeStruct(dims, kind)


def sigmoid(value):
    return 1.0 / (1.0 + jnp.exp(-value))


def pack_kernel(place_ref, rows_ref, gain_ref, match_ref, out_ref):
    at = lax.broadcasted_iota(jnp.int32, (8, 128), 0)
    terms = jnp.zeros((8, 128), F32)
    for r in range(8):
        unit = place_ref[0] * 8 + r
        tile = gain_ref[pl.ds(jnp.minimum(unit // 3, D // 128 - 1), 1), :]
        high = tile.astype(BF16).astype(F32)
        middle = (tile - high).astype(BF16).astype(F32)
        which = lax.rem(unit, 3)
        term = jnp.where(which == 0, high, jnp.where(which == 1, middle, tile - high - middle))
        terms = jnp.where(at == r, term, terms)
    out_ref[:, :D] = rows_ref[...]
    out_ref[:, D : D + 128] = terms.astype(BF16)
    out_ref[:, D + 128 :] = jnp.zeros((8, 128), BF16)
    match_row = match_ref[...].astype(F32)
    out_ref[:, D + 128 : D + 128 + N_PEER] = jnp.broadcast_to(match_row, (8, N_PEER)).astype(BF16)


def pack(place, rows, gain_tiles, match_row):
    return pl.pallas_call(
        pack_kernel,
        out_shape=shape((8, PACKED)),
        in_specs=[SMEM] + [VMEM] * 3,
        out_specs=VMEM,
        compiler_params=ROOM,
        name="pack",
    )(place, rows, gain_tiles, match_row)


def landed_rows(landed_ref, z, at):
    pieces = [landed_ref[y * 16 + z * 4 + x, :, at : at + WIDE].astype(F32) for y in range(NY) for x in range(NX)]
    return jnp.concatenate(pieces, axis=0)


CHUNKS = [(z, at, slice(z * SPAN + at, z * SPAN + at + WIDE)) for z in range(NZ) for at in range(0, SPAN, WIDE)]


def weights(both_ref, cols):
    return both_ref[:, HALF + cols.start : HALF + cols.stop]


def adapter_kernel(landed_ref, both_ref, grad_ref, active_ref, part_ref, normed_ref):
    terms = both_ref[:, HALF + D : HALF + D + 128].astype(F32)
    squares = jnp.zeros((ROWS, 1), F32)
    for z, at, cols in CHUNKS:
        t = landed_rows(landed_ref, z, at)
        squares += jnp.sum(t * t, axis=1, keepdims=True)
    inv_rms = lax.rsqrt(squares / D + 1e-05)
    product = jnp.zeros((ROWS, 2 * LATENT), F32)
    for z, at, cols in CHUNKS:
        tiles = range(cols.start // 128, cols.stop // 128)
        gain = [jnp.sum(terms[3 * t : 3 * t + 3], axis=0, keepdims=True) for t in tiles]
        gain = jnp.concatenate(gain, axis=1)
        n = (landed_rows(landed_ref, z, at) * inv_rms * gain).astype(BF16)
        normed_ref[:, cols] = n
        product += lax.dot_general(n, weights(both_ref, cols), LAST, preferred_element_type=F32)
    lane = lax.broadcasted_iota(jnp.int32, (ROWS, 2 * LATENT), 1)
    is_up = lax.rem(lane, 8) < 4
    preact = jnp.where(is_up, 0.0, product)
    q = sigmoid(preact)
    active = pltpu.roll(preact * q, 2 * LATENT - 4, 1)
    active = jnp.where(is_up, active, 0.0).astype(BF16)
    active_ref[...] = active
    act_grad = jnp.zeros((ROWS, 2 * LATENT), F32)
    for z, at, cols in CHUNKS:
        act_grad += lax.dot_general(grad_ref[:, cols], weights(both_ref, cols), LAST, preferred_element_type=F32)
    act_grad = pltpu.roll(act_grad, 4, 1)
    pre_grad = jnp.where(is_up, 0.0, act_grad * q * (1.0 + preact * (1.0 - q)))
    down = pre_grad.T.astype(BF16)
    up = active.astype(F32).T.astype(BF16)
    for j in range(D // WIDE):
        cols = slice(j * WIDE, (j + 1) * WIDE)
        part = jnp.dot(down, normed_ref[:, cols], preferred_element_type=F32)
        part += jnp.dot(up, grad_ref[:, cols], preferred_element_type=F32)
        part = part.T.astype(BF16)
        for i in range(WIDE // OWN):
            p = j * (WIDE // OWN) + i
            y, z, x = p // 16, (p // 4) % 4, p % 4
            part_ref[y * NX + x, z * OWN : (z + 1) * OWN, :] = part[i * OWN : (i + 1) * OWN]


def adapter(landed, both, held_grad):
    return pl.pallas_call(
        adapter_kernel,
        out_shape=(shape((ROWS, 2 * LATENT)), shape((PLANE, NZ * OWN, 2 * LATENT))),
        in_specs=[VMEM] * 3,
        out_specs=[VMEM] * 2,
        scratch_shapes=[pltpu.VMEM((ROWS, D), BF16)],
        compiler_params=ROOM,
        name="adapter",
    )(landed, both, held_grad)


def finish_kernel(landed_ref, both_ref, active_ref, out_ref, zero_ref):
    zero_ref[...] = jnp.zeros(zero_ref.shape, F32)
    for z, at, cols in CHUNKS:
        up = jnp.dot(active_ref[...], weights(both_ref, cols), preferred_element_type=F32)
        t = landed_rows(landed_ref, z, at) + up
        for g in range(PLANE):
            out_ref[g, :, cols] = t[g * 8 : (g + 1) * 8].astype(BF16)


def finish(landed, both, active):
    return pl.pallas_call(
        finish_kernel,
        out_shape=(shape((PLANE, 8, D)), shape((8, 2 * LATENT), F32)),
        in_specs=[VMEM] * 3,
        out_specs=[VMEM] * 2,
        compiler_params=ROOM,
        name="finish",
    )(landed, both, active)


def beside_kernel(a0, a1, packed_ref, out_ref):
    out_ref[:, :, :SPAN] = a0[...]
    out_ref[:, :, SPAN:HALF] = a1[...]
    for g in range(PLANE):
        out_ref[g, :, HALF:] = packed_ref[...]


def beside(a_parts, packed):
    return pl.pallas_call(
        beside_kernel,
        out_shape=shape((PLANE, 8, HALF + PACKED)),
        in_specs=[VMEM] * 3,
        out_specs=VMEM,
        compiler_params=ROOM,
        name="beside",
    )(*a_parts, packed)


def seen_kernel(*refs):
    refs[-1][...] = sum(ref[(0,) * (len(ref.shape) - 2) + (slice(0, 8), slice(0, 128))].astype(F32) for ref in refs[:-1])


def seen(*values):
    return pl.pallas_call(
        seen_kernel,
        out_shape=shape((8, 128), F32),
        in_specs=[VMEM] * len(values),
        out_specs=VMEM,
        compiler_params=ROOM,
        cost_estimate=pl.CostEstimate(flops=LEAD, bytes_accessed=0, transcendentals=0),
        name="seen",
    )(*values)


def halves_kernel(spread_ref, after_ref, b0, b1):
    b0[...] = spread_ref[:, :, :SPAN]
    b1[...] = spread_ref[:, :, SPAN:]


def halves(spread_b, after):
    return pl.pallas_call(
        halves_kernel,
        out_shape=[shape((PLANE, 8, SPAN))] * 2,
        in_specs=[VMEM] * 2,
        out_specs=[VMEM] * 2,
        compiler_params=ROOM,
        name="halves",
    )(spread_b, after)


def route_kernel(z_ref, before_ref, a_ref, b0, b1, after_ref, out_ref):
    z = z_ref[0]
    for k in range(NZ):
        plane = lax.rem(z + NZ - k, NZ) * NX
        for xy in range(PLANE):
            piece = a_ref[xy, :, k * SPAN : (k + 1) * SPAN] if k < 2 else (b0, b1)[k - 2][xy]
            out_ref[before_ref[plane + (xy // NX) * 16 + xy % NX]] = piece


def route(z_at, match_before, spread_a, b_parts, after):
    return pl.pallas_call(
        route_kernel,
        out_shape=shape((N_PEER, 8, SPAN)),
        in_specs=[SMEM] * 2 + [VMEM] * 4,
        out_specs=VMEM,
        compiler_params=ROOM,
        name="route",
    )(z_at, match_before, spread_a, *b_parts, after)


def sums_kernel(p0, down_rows_ref, gain_ref, down_ref, up_ref, grad_gain_ref):
    total = p0[...].T
    for g in range(PLANE):
        up_ref[g * 4 : (g + 1) * 4, :] = total[g * 8 : g * 8 + 4]
        down_ref[g * 4 : (g + 1) * 4, :] = total[g * 8 + 4 : (g + 1) * 8]
    weighted = down_rows_ref[...].astype(F32) * down_ref[...]
    grad_gain_ref[...] = jnp.sum(weighted, axis=0, keepdims=True) / gain_ref[...]


def sums(parts, own_down, own_gain):
    return pl.pallas_call(
        sums_kernel,
        out_shape=(shape((LATENT, OWN), F32), shape((LATENT, OWN), F32), shape((1, OWN), F32)),
        in_specs=[VMEM] * 3,
        out_specs=[VMEM] * 3,
        compiler_params=ROOM,
        name="sums",
    )(*parts, own_down, own_gain)


def on_device(hidden_in, out_grad, gain, w_down, w_up, matching):
    tokens, held_grad = hidden_in[0], out_grad[0]
    down_rows, up_rows = w_down[0], w_up[0]
    peer = lax.axis_index("peer")
    z = (peer // NX) % NZ
    place = (peer // 16) * NX + peer % NX

    z_at = z.reshape(1)
    out = [lax.dynamic_slice_in_dim(tokens, ((z + k) % NZ) * SPAN, SPAN, 1).reshape(PLANE, 8, SPAN) for k in range(NZ)]
    a_parts = [along(out[k], 1, k) for k in (0, 1)]
    spread_b = in_plane(jnp.concatenate(out[2:], axis=2))

    rows = lambda array: lax.dynamic_slice_in_dim(array, place * 4, 4, 0)
    both_rows = jnp.concatenate([rows(up_rows), rows(down_rows)], axis=0)
    packed = along(pack(place.reshape(1), both_rows, gain.reshape(D // 128, 128), matching), 1)
    match_before = packed[0, D + 128 : D + 128 + N_PEER].astype(jnp.int32)

    b_parts = [along(part, 1, k) for k, part in zip((2, 3), halves(spread_b, seen(a_parts[0], packed)))]
    spread_a = in_plane(beside(a_parts, packed))
    both = spread_a.reshape(ROWS, HALF + PACKED)

    landed = in_cube(route(z_at, match_before, spread_a, b_parts, seen(*b_parts)))
    active, part = adapter(landed, both, held_grad)
    act_out, zero = finish(landed, both, active)

    part = in_plane(part)
    plane_sum = jnp.sum(part.astype(F32), axis=0).reshape(NZ, OWN, 2 * LATENT)
    lines = lax.all_to_all(plane_sum, "peer", split_axis=0, concat_axis=0, tiled=True, axis_index_groups=LINES)
    parts = [along(jnp.sum(lines, axis=0) + zero[:1], -1)]
    own = lambda array: lax.dynamic_slice_in_dim(array, peer * OWN, OWN, 1)
    grad_down, grad_up, grad_gain = sums(parts, own(down_rows), own(gain))
    return act_out.reshape(1, ROWS, D), grad_down[None], grad_up[None], grad_gain


def solution(mesh):
    placed = (
        P("section", "peer", None),
        P("section", "peer", None),
        P("section", None),
        P("section", None, None),
        P("section", None, None),
        P("section", None),
    )
    return jax.shard_map(
        on_device,
        mesh=mesh,
        in_specs=placed,
        out_specs=(
            P("section", "peer", None),
            P("section", None, "peer"),
            P("section", None, "peer"),
            P("section", "peer"),
        ),
        check_vma=False,
    )
```

```python
import jax
import jax.numpy as jnp
from jax import lax
from jax.experimental import pallas as pl
from jax.experimental.pallas import tpu as pltpu
from jax.sharding import PartitionSpec as P

NX, NY, NZ = 4, 4, 4
N_PEER = NX * NY * NZ
N_SECTION = 8
PLANE = NX * NY
D = 5120
LATENT = 64
ROWS = 128
WIDE = 640
SPAN = D // NZ
HALF = 2 * SPAN
LEAD = 10**11
PACKED = D + 256
FIRST, SECOND = (3, 0), (1, 2)
OWN = D // N_PEER
PLANES = [[y * 16 + z * 4 + x for y in range(NY) for x in range(NX)] for z in range(NZ)]
LINES = [[y * 16 + z * 4 + x for z in range(NZ)] for y in range(NY) for x in range(NX)]
BF16, F32 = jnp.bfloat16, jnp.float32
SMEM = pl.BlockSpec(memory_space=pltpu.SMEM)
VMEM = pl.BlockSpec(memory_space=pltpu.VMEM)
ROOM = pltpu.CompilerParams(vmem_limit_bytes=16 * 1024 * 1024)
LAST = (((1,), (1,)), ((), ()))


def along(value, section_steps, z_steps=0):
    pairs = []
    for s in range(N_SECTION):
        for y in range(NY):
            for z in range(NZ):
                for x in range(NX):
                    source = s * N_PEER + y * 16 + z * 4 + x
                    target = ((s + section_steps) % N_SECTION) * N_PEER + y * 16 + ((z + z_steps) % NZ) * 4 + x
                    pairs.append((source, target))
    return lax.ppermute(value, ("section", "peer"), pairs)


def in_plane(value):
    return lax.all_to_all(value, "peer", split_axis=0, concat_axis=0, tiled=True, axis_index_groups=PLANES)


def in_cube(value):
    return lax.all_to_all(value, "peer", split_axis=0, concat_axis=0, tiled=True)


def shape(dims, kind=BF16):
    return jax.ShapeDtypeStruct(dims, kind)


def sigmoid(value):
    return 1.0 / (1.0 + jnp.exp(-value))


def pack_kernel(place_ref, rows_ref, gain_ref, match_ref, out_ref):
    at = lax.broadcasted_iota(jnp.int32, (8, 128), 0)
    terms = jnp.zeros((8, 128), F32)
    for r in range(8):
        unit = place_ref[0] * 8 + r
        tile = gain_ref[pl.ds(jnp.minimum(unit // 3, D // 128 - 1), 1), :]
        high = tile.astype(BF16).astype(F32)
        middle = (tile - high).astype(BF16).astype(F32)
        which = lax.rem(unit, 3)
        term = jnp.where(which == 0, high, jnp.where(which == 1, middle, tile - high - middle))
        terms = jnp.where(at == r, term, terms)
    out_ref[:, :D] = rows_ref[...]
    out_ref[:, D : D + 128] = terms.astype(BF16)
    out_ref[:, D + 128 :] = jnp.zeros((8, 128), BF16)
    match_row = match_ref[...].astype(F32)
    out_ref[:, D + 128 : D + 128 + N_PEER] = jnp.broadcast_to(match_row, (8, N_PEER)).astype(BF16)


def pack(place, rows, gain_tiles, match_row):
    return pl.pallas_call(
        pack_kernel,
        out_shape=shape((8, PACKED)),
        in_specs=[SMEM] + [VMEM] * 3,
        out_specs=VMEM,
        compiler_params=ROOM,
        name="pack",
    )(place, rows, gain_tiles, match_row)


def landed_rows(landed_ref, z, at):
    pieces = [landed_ref[y * 16 + z * 4 + x, :, at : at + WIDE].astype(F32) for y in range(NY) for x in range(NX)]
    return jnp.concatenate(pieces, axis=0)


CHUNKS = [(z, at, slice(z * SPAN + at, z * SPAN + at + WIDE)) for z in range(NZ) for at in range(0, SPAN, WIDE)]


def weights(both_ref, cols):
    return both_ref[:, HALF + cols.start : HALF + cols.stop]


def adapter_kernel(landed_ref, both_ref, grad_ref, active_ref, part_ref, normed_ref):
    terms = both_ref[:, HALF + D : HALF + D + 128].astype(F32)
    squares = jnp.zeros((ROWS, 1), F32)
    for z, at, cols in CHUNKS:
        t = landed_rows(landed_ref, z, at)
        squares += jnp.sum(t * t, axis=1, keepdims=True)
    inv_rms = lax.rsqrt(squares / D + 1e-05)
    product = jnp.zeros((ROWS, 2 * LATENT), F32)
    for z, at, cols in CHUNKS:
        tiles = range(cols.start // 128, cols.stop // 128)
        gain = [jnp.sum(terms[3 * t : 3 * t + 3], axis=0, keepdims=True) for t in tiles]
        gain = jnp.concatenate(gain, axis=1)
        n = (landed_rows(landed_ref, z, at) * inv_rms * gain).astype(BF16)
        normed_ref[:, cols] = n
        product += lax.dot_general(n, weights(both_ref, cols), LAST, preferred_element_type=F32)
    lane = lax.broadcasted_iota(jnp.int32, (ROWS, 2 * LATENT), 1)
    is_up = lax.rem(lane, 8) < 4
    preact = jnp.where(is_up, 0.0, product)
    q = sigmoid(preact)
    active = pltpu.roll(preact * q, 2 * LATENT - 4, 1)
    active = jnp.where(is_up, active, 0.0).astype(BF16)
    active_ref[...] = active
    act_grad = jnp.zeros((ROWS, 2 * LATENT), F32)
    for z, at, cols in CHUNKS:
        act_grad += lax.dot_general(grad_ref[:, cols], weights(both_ref, cols), LAST, preferred_element_type=F32)
    act_grad = pltpu.roll(act_grad, 4, 1)
    pre_grad = jnp.where(is_up, 0.0, act_grad * q * (1.0 + preact * (1.0 - q)))
    down = pre_grad.T.astype(BF16)
    up = active.astype(F32).T.astype(BF16)
    for j in range(D // WIDE):
        cols = slice(j * WIDE, (j + 1) * WIDE)
        part = jnp.dot(down, normed_ref[:, cols], preferred_element_type=F32)
        part += jnp.dot(up, grad_ref[:, cols], preferred_element_type=F32)
        part = part.T.astype(BF16)
        for i in range(WIDE // OWN):
            p = j * (WIDE // OWN) + i
            y, z, x = p // 16, (p // 4) % 4, p % 4
            part_ref[y * NX + x, z * OWN : (z + 1) * OWN, :] = part[i * OWN : (i + 1) * OWN]


def adapter(landed, both, held_grad):
    return pl.pallas_call(
        adapter_kernel,
        out_shape=(shape((ROWS, 2 * LATENT)), shape((PLANE, NZ * OWN, 2 * LATENT))),
        in_specs=[VMEM] * 3,
        out_specs=[VMEM] * 2,
        scratch_shapes=[pltpu.VMEM((ROWS, D), BF16)],
        compiler_params=ROOM,
        name="adapter",
    )(landed, both, held_grad)


def finish_kernel(landed_ref, both_ref, active_ref, out_ref, zero_ref):
    zero_ref[...] = jnp.zeros(zero_ref.shape, F32)
    for z, at, cols in CHUNKS:
        up = jnp.dot(active_ref[...], weights(both_ref, cols), preferred_element_type=F32)
        t = landed_rows(landed_ref, z, at) + up
        for g in range(PLANE):
            out_ref[g, :, cols] = t[g * 8 : (g + 1) * 8].astype(BF16)


def finish(landed, both, active):
    return pl.pallas_call(
        finish_kernel,
        out_shape=(shape((PLANE, 8, D)), shape((8, 2 * LATENT), F32)),
        in_specs=[VMEM] * 3,
        out_specs=[VMEM] * 2,
        compiler_params=ROOM,
        name="finish",
    )(landed, both, active)


def beside_kernel(a0, a1, packed_ref, out_ref):
    out_ref[:, :, :SPAN] = a0[...]
    out_ref[:, :, SPAN:HALF] = a1[...]
    for g in range(PLANE):
        out_ref[g, :, HALF:] = packed_ref[...]


def beside(a_parts, packed):
    return pl.pallas_call(
        beside_kernel,
        out_shape=shape((PLANE, 8, HALF + PACKED)),
        in_specs=[VMEM] * 3,
        out_specs=VMEM,
        compiler_params=ROOM,
        name="beside",
    )(*a_parts, packed)


def seen_kernel(*refs):
    refs[-1][...] = sum(ref[(0,) * (len(ref.shape) - 2) + (slice(0, 8), slice(0, 128))].astype(F32) for ref in refs[:-1])


def seen(*values):
    return pl.pallas_call(
        seen_kernel,
        out_shape=shape((8, 128), F32),
        in_specs=[VMEM] * len(values),
        out_specs=VMEM,
        compiler_params=ROOM,
        cost_estimate=pl.CostEstimate(flops=LEAD, bytes_accessed=0, transcendentals=0),
        name="seen",
    )(*values)


def halves_kernel(spread_ref, after_ref, b0, b1):
    b0[...] = spread_ref[:, :, :SPAN]
    b1[...] = spread_ref[:, :, SPAN:]


def halves(spread_b, after):
    return pl.pallas_call(
        halves_kernel,
        out_shape=[shape((PLANE, 8, SPAN))] * 2,
        in_specs=[VMEM] * 2,
        out_specs=[VMEM] * 2,
        compiler_params=ROOM,
        name="halves",
    )(spread_b, after)


def route_kernel(z_ref, before_ref, a_ref, b0, b1, after_ref, out_ref):
    z = z_ref[0]
    for i, k in enumerate(FIRST + SECOND):
        plane = lax.rem(z + NZ - k, NZ) * NX
        for xy in range(PLANE):
            piece = a_ref[xy, :, i * SPAN : (i + 1) * SPAN] if i < 2 else (b0, b1)[i - 2][xy]
            out_ref[before_ref[plane + (xy // NX) * 16 + xy % NX]] = piece


def route(z_at, match_before, spread_a, b_parts, after):
    return pl.pallas_call(
        route_kernel,
        out_shape=shape((N_PEER, 8, SPAN)),
        in_specs=[SMEM] * 2 + [VMEM] * 4,
        out_specs=VMEM,
        compiler_params=ROOM,
        name="route",
    )(z_at, match_before, spread_a, *b_parts, after)


def sums_kernel(p0, down_rows_ref, gain_ref, down_ref, up_ref, grad_gain_ref):
    total = p0[...].T
    for g in range(PLANE):
        up_ref[g * 4 : (g + 1) * 4, :] = total[g * 8 : g * 8 + 4]
        down_ref[g * 4 : (g + 1) * 4, :] = total[g * 8 + 4 : (g + 1) * 8]
    weighted = down_rows_ref[...].astype(F32) * down_ref[...]
    grad_gain_ref[...] = jnp.sum(weighted, axis=0, keepdims=True) / gain_ref[...]


def sums(parts, own_down, own_gain):
    return pl.pallas_call(
        sums_kernel,
        out_shape=(shape((LATENT, OWN), F32), shape((LATENT, OWN), F32), shape((1, OWN), F32)),
        in_specs=[VMEM] * 3,
        out_specs=[VMEM] * 3,
        compiler_params=ROOM,
        name="sums",
    )(*parts, own_down, own_gain)


def on_device(hidden_in, out_grad, gain, w_down, w_up, matching):
    tokens, held_grad = hidden_in[0], out_grad[0]
    down_rows, up_rows = w_down[0], w_up[0]
    peer = lax.axis_index("peer")
    z = (peer // NX) % NZ
    place = (peer // 16) * NX + peer % NX

    z_at = z.reshape(1)
    out = [lax.dynamic_slice_in_dim(tokens, ((z + k) % NZ) * SPAN, SPAN, 1).reshape(PLANE, 8, SPAN) for k in FIRST + SECOND]
    a_parts = [along(out[i], 1, k) for i, k in enumerate(FIRST)]
    spread_b = in_plane(jnp.concatenate(out[2:], axis=2))

    rows = lambda array: lax.dynamic_slice_in_dim(array, place * 4, 4, 0)
    both_rows = jnp.concatenate([rows(up_rows), rows(down_rows)], axis=0)
    packed = along(pack(place.reshape(1), both_rows, gain.reshape(D // 128, 128), matching), 1)
    match_before = packed[0, D + 128 : D + 128 + N_PEER].astype(jnp.int32)

    b_parts = [along(part, 1, k) for k, part in zip(SECOND, halves(spread_b, seen(a_parts[0], packed)))]
    spread_a = in_plane(beside(a_parts, packed))
    both = spread_a.reshape(ROWS, HALF + PACKED)

    landed = in_cube(route(z_at, match_before, spread_a, b_parts, seen(*b_parts)))
    active, part = adapter(landed, both, held_grad)
    act_out, zero = finish(landed, both, active)

    part = in_plane(part)
    plane_sum = jnp.sum(part.astype(F32), axis=0).reshape(NZ, OWN, 2 * LATENT)
    lines = lax.all_to_all(plane_sum, "peer", split_axis=0, concat_axis=0, tiled=True, axis_index_groups=LINES)
    parts = [along(jnp.sum(lines, axis=0) + zero[:1], -1)]
    own = lambda array: lax.dynamic_slice_in_dim(array, peer * OWN, OWN, 1)
    grad_down, grad_up, grad_gain = sums(parts, own(down_rows), own(gain))
    return act_out.reshape(1, ROWS, D), grad_down[None], grad_up[None], grad_gain


def solution(mesh):
    placed = (
        P("section", "peer", None),
        P("section", "peer", None),
        P("section", None),
        P("section", None, None),
        P("section", None, None),
        P("section", None),
    )
    return jax.shard_map(
        on_device,
        mesh=mesh,
        in_specs=placed,
        out_specs=(
            P("section", "peer", None),
            P("section", None, "peer"),
            P("section", None, "peer"),
            P("section", "peer"),
        ),
        check_vma=False,
    )
```
